32 devices in a mesh: group: 4 (over y, core), vocab: 8 (over z, x).
Axes of the slice: x: 2, y: 2, z: 4, core: 2. Of those that a mesh axis runs over, the one named last changes fastest.
Arguments:
- hidden: bfloat16 [16, 2560], P('group', 'vocab'), as said below
- dealt_slot: int32 [16], P('group'), may hold values from 0 to 15, as said below
- targets: int32 [16], P('group'), may hold values from 0 to 16383
- final_gain: float32 [2560], replicated, may hold values from 0.5 to 1.5
- vocab_head: bfloat16 [16384, 2560], P(('group', 'vocab')), as said below
- first_gain: float32 [2560], replicated, may hold values from 0.25 to 1.75
- qkv_weight: bfloat16 [2560, 3072], P(None, 'vocab'), may hold values from -0.125 to 0.125
Outputs:
- logprob: float32 [16], P('group')
- entropy: float32 [16], P('group')
- qkv_out: bfloat16 [3072, 16], P('vocab', 'group')
The draws below stay inside these ranges and needn't reach their ends.
Inputs may be any that keep to these rules, and one draw needn't show every extreme that they name: dealt_slot is a permutation of the 16 slots; position r is owned by group r // 4, slot s belongs to group s // 4, and the positions owned by each group go exactly 1 to every group. `vocab_head`: independent rows, none zero. `hidden`: independent rows, none zero.
All inputs are finite; a program needn't handle non-finite values.
Results may differ from the reference program's by a relative error of at most 0.001.
The reference program's roundings to bfloat16 on the way (of `dealt`, `normed` and `first_normed`) count: a program that leaves them out, or rounds other values in their place, can miss the bound.
Values may be sent and summed in bfloat16 or wider, within the bound.
A program may use at most 64 MiB of HBM per device.

```python
import math
import jax
import jax.numpy as jnp
import numpy as np
from jax import lax

D = 2560
QUOTA = 1
QKV = 3072
VOCAB = 16384
ROW_GROUP = 4
ROWS = 16
N_GROUP = 4


def pair_rows(key):
    inner = jax.random.fold_in(key, 7)
    key_ids, key_rows = jax.random.split(inner, 2)
    first_ids = jax.random.permutation(key_ids, VOCAB // 2)[:6].astype(jnp.int32)
    second_ids = first_ids + VOCAB // 2
    strength = jnp.array([4.0, 3.0, 2.2, 4.0, 3.0, 2.2], jnp.float32)
    base_rows = jnp.clip(jax.random.normal(key_rows, (6, D), jnp.float32), -5.0, 5.0) * (5.0 / math.sqrt(D)) * strength[:, None]
    return (first_ids, second_ids, base_rows)


def draw_vocab_head(key, part):
    inner = jax.random.fold_in(key, 3)
    key_scale, key_vals = jax.random.split(inner, 2)
    row_scale = jnp.exp(jax.random.uniform(key_scale, (VOCAB, 1), jnp.float32, math.log(0.4), math.log(4.0)))
    values = jnp.clip(jax.random.normal(key_vals, (VOCAB, D), jnp.float32), -5.0, 5.0)
    values = values * row_scale * (5.0 / math.sqrt(D))
    first_ids, second_ids, base_rows = pair_rows(key)
    values = values.at[first_ids].set(base_rows)
    values = values.at[second_ids].set(jnp.roll(base_rows, 1, axis=1))
    return values.astype(jnp.bfloat16)


def draw_hidden(key, part):
    inner = jax.random.fold_in(key, 5)
    key_rows, key_cols, key_vals = jax.random.split(inner, 3)
    row_scale = jnp.exp(jax.random.uniform(key_rows, (ROWS, 1), jnp.float32, 0.0, math.log(10.0))) * 0.3
    col_scale = jnp.exp(jax.random.uniform(key_cols, (1, D), jnp.float32, math.log(0.5), math.log(5.0)))
    values = jnp.clip(jax.random.normal(key_vals, (ROWS, D), jnp.float32), -5.0, 5.0) * row_scale * col_scale
    return values.astype(jnp.bfloat16)


def draw_dealt_slot(key, part):
    inner = jax.random.fold_in(key, 9)
    key_send, key_recv = jax.random.split(inner, 2)

    def one_order(single):
        return jax.random.permutation(single, ROW_GROUP).astype(jnp.int32)
    send_order = jax.vmap(one_order)(jax.random.split(key_send, N_GROUP))
    recv_order = jax.vmap(one_order)(jax.random.split(key_recv, N_GROUP))
    target_group = send_order // QUOTA
    send_rank = send_order % QUOTA
    sender = jnp.arange(N_GROUP, dtype=jnp.int32)[:, None]
    arrival = sender * QUOTA + send_rank
    local_slot = recv_order[target_group, arrival]
    dealt = target_group * ROW_GROUP + local_slot
    return dealt.reshape(ROWS).astype(jnp.int32)


def plant(values, rng, least, top_value):
    shape = values.shape
    place = [jax.random.randint(jax.random.fold_in(rng, axis), (), 0, shape[axis]) for axis in range(len(shape))]
    values = values.at[tuple(place)].set(least)
    longest = shape.index(max(shape))
    place[longest] = (place[longest] + 1) % shape[longest]
    return values.at[tuple(place)].set(top_value)


def block_scale(rng, shape, shards, low, high):
    factor_of = 1.0
    for dim, parts in shards:
        heights = jax.random.uniform(jax.random.fold_in(jax.random.fold_in(rng, 6), dim), (parts,), jnp.float32, low / len(shards), high / len(shards))
        factor_of = factor_of * jnp.repeat(jnp.exp(heights), shape[dim] // parts).reshape((-1,) + (1,) * (len(shape) - 1 - dim))
    return factor_of


def rank_table(count, lean):
    weights = [(1 << 20) // math.isqrt(rank ** lean) + 1 for rank in range(1, count + 1)]
    deviation = 1 + sum(weights) // (1 << 30)
    return np.cumsum(np.array([max(1, weight // deviation) for weight in weights]))


def ranked_ids(rng, extent, amount, slope):
    table = rank_table(amount, slope)
    ticket = jax.random.randint(jax.random.fold_in(rng, 1), extent, 0, int(table[amount - 1]))
    standing = jnp.searchsorted(jnp.asarray(table, jnp.int32), ticket, side="right")
    return jax.random.permutation(jax.random.fold_in(rng, 2), amount)[standing].astype(jnp.int32)


def gaussian(rng, dims, spread, bound, shards=(), kind=jnp.bfloat16):
    drawn = jax.random.normal(rng, dims, jnp.float32) * spread
    if len(shards) > 0:
        drawn = block_scale(rng, dims, shards, -0.22, 0.18) * drawn
    return jnp.clip(drawn, min=-bound, max=bound).astype(kind)


def setup_inputs(seed: int = 0) -> dict:
    key_list = jax.random.split(jax.random.key(seed), 8)
    return {
        "hidden": draw_hidden(jax.random.fold_in(key_list[7], 71), 0),
        "dealt_slot": draw_dealt_slot(jax.random.fold_in(key_list[7], 71), 0),
        "targets": plant(ranked_ids(key_list[2], (ROWS,), VOCAB, 2), jax.random.fold_in(key_list[2], 3), 0, VOCAB - 1).astype(jnp.int32),
        "final_gain": jnp.clip(1.0 + 0.1 * jax.random.normal(key_list[3], (D,), jnp.float32), 0.5, 1.5),
        "vocab_head": draw_vocab_head(jax.random.fold_in(key_list[7], 71), 0),
        "first_gain": jnp.clip(1.0 + 0.15 * jax.random.normal(key_list[5], (D,), jnp.float32), 0.25, 1.75),
        "qkv_weight": gaussian(key_list[6], (D, QKV), D ** -0.5, 0.125, ((1, 8),)),
    }


eps = 1e-06

def rms_scaled(values, gain):
    wide = values.astype(jnp.float32)
    factor = lax.rsqrt(lax.optimization_barrier(jnp.mean(wide * wide, axis=-1, keepdims=True)) + eps)
    return (wide * factor * gain).astype(jnp.bfloat16)

def reference(hidden, dealt_slot, targets, final_gain, vocab_head, first_gain, qkv_weight):
    dealt = jnp.zeros_like(hidden).at[dealt_slot].set(hidden)
    dealt_targets = jnp.zeros_like(targets).at[dealt_slot].set(targets)
    blocks = ROWS // ROW_GROUP
    head_wide = vocab_head.astype(jnp.float32)

    def score(pair):
        rows, wanted = pair
        normed = rms_scaled(rows, final_gain)
        logits = jnp.einsum('rd,vd->rv', normed.astype(jnp.float32), head_wide)
        row_top = lax.optimization_barrier(jnp.max(logits, axis=1))
        shifted = logits - row_top[:, None]
        expons = jnp.exp(shifted)
        row_total = lax.optimization_barrier(jnp.sum(expons, axis=1))
        row_weighted = lax.optimization_barrier(jnp.sum(expons * shifted, axis=1))
        picked = jnp.take_along_axis(logits, wanted[:, None].astype(jnp.int32), axis=1)[:, 0]
        log_total = jnp.log(row_total)
        return (picked - row_top - log_total, log_total - row_weighted / row_total)
    dealt_logprob, dealt_entropy = lax.map(score, (dealt.reshape(blocks, ROW_GROUP, D), dealt_targets.reshape(blocks, ROW_GROUP)))
    dealt_logprob = dealt_logprob.reshape(ROWS)
    dealt_entropy = dealt_entropy.reshape(ROWS)
    logprob = dealt_logprob[dealt_slot]
    entropy = dealt_entropy[dealt_slot]
    embedded = vocab_head[dealt_targets].astype(jnp.float32)
    first_normed = rms_scaled(embedded, first_gain)
    projected = jnp.einsum('rd,dc->cr', first_normed.astype(jnp.float32), qkv_weight.astype(jnp.float32))
    return (logprob, entropy, projected.astype(jnp.bfloat16))
```

```python
import functools

import jax
import jax.numpy as jnp
from jax import lax
from jax.experimental import pallas as pl
from jax.experimental.pallas import tpu as pltpu
from jax.sharding import PartitionSpec as P

eps = 1e-06
MESH = pl.DeviceIdType.MESH
LANES = 128
UNROLL_MAX = 32


def each(first, last, body):
    if last - first <= UNROLL_MAX:
        for k in range(first, last):
            body(k)
    else:

        def step(k, carry):
            body(k)
            return carry

        lax.fori_loop(first, last, step, 0)


def rms_scaled(wide, gain):
    factor = lax.rsqrt(jnp.mean(wide * wide, axis=-1, keepdims=True) + eps)
    return (wide * factor * gain).astype(jnp.bfloat16)


def merged(ref):
    tops = ref[:, 0:1, :]
    totals = ref[:, 1:2, :]
    top = jnp.max(tops, axis=0, keepdims=True)
    gap = tops - top
    scale = jnp.exp(gap)
    total = jnp.sum(scale * totals, axis=0)
    weighted = jnp.sum(scale * (ref[:, 2:3, :] + totals * gap), axis=0)
    target = jnp.sum(ref[:, 3:4, :], axis=0)
    return top[0], total, weighted, target


def put_stats(ref, k, stats):
    for row, stat in enumerate(stats):
        ref[k, row : row + 1, :] = stat


def kernel(
    groups,
    shards,
    starts,
    width,
    hidden_ref,
    slot_ref,
    target_ref,
    final_gain_ref,
    head_hbm,
    first_gain_ref,
    qkv_hbm,
    logprob_ref,
    entropy_ref,
    out_ref,
    head,
    qkv,
    ids,
    pieces,
    wide_rows,
    normed,
    rows_all,
    picked,
    picked_out,
    picked_in,
    summed,
    embedded,
    stats_one,
    stats_two,
    local_sem,
    send_sem,
    recv_sem,
):
    group = lax.axis_index("group")
    shard = lax.axis_index("vocab")
    row_group, cols = hidden_ref.shape
    rows = row_group * groups
    vocab_dev, width_all = head.shape
    tiles = width_all // LANES
    devices = groups * shards
    me = group * shards + shard
    span = width * LANES

    head_copy = pltpu.make_async_copy(head_hbm, head, local_sem.at[0])
    qkv_copy = pltpu.make_async_copy(qkv_hbm, qkv, local_sem.at[1])
    head_copy.start()
    qkv_copy.start()

    def group_peer(k):
        return (lax.rem(group + k, groups), shard)

    def shard_peer(k):
        return (group, lax.rem(shard + k, shards))

    def send(src, dst, phase, peer):
        pltpu.make_async_remote_copy(
            src_ref=src,
            dst_ref=dst,
            send_sem=send_sem.at[phase],
            recv_sem=recv_sem.at[phase],
            device_id=peer,
            device_id_type=MESH,
        ).start()

    def wait_all(ref, count, sem):
        if count > 0:
            part = ref.at[pl.ds(0, count)]
            pltpu.make_async_copy(part, part, sem).wait()

    barrier = pltpu.get_barrier_semaphore()
    each(1, groups, lambda k: pl.semaphore_signal(barrier, inc=1, device_id=group_peer(k), device_id_type=MESH))
    each(1, shards, lambda k: pl.semaphore_signal(barrier, inc=1, device_id=shard_peer(k), device_id_type=MESH))
    ids[group, 0:1, 0:row_group] = slot_ref[...]
    ids[group, 1:2, 0:row_group] = target_ref[...]
    pl.semaphore_wait(barrier, groups + shards - 2)

    each(1, groups, lambda k: send(ids.at[group], ids.at[group], 0, group_peer(k)))
    each(1, shards, lambda k: send(hidden_ref, pieces.at[shard], 1, shard_peer(k)))
    pieces[shard] = hidden_ref[...]

    wait_all(pieces, shards - 1, recv_sem.at[1])
    for v in range(shards):
        wide_rows[:, v * cols : (v + 1) * cols] = pieces[v].astype(jnp.float32)
    normed[group] = rms_scaled(wide_rows[...], final_gain_ref[...])
    each(1, groups, lambda k: send(normed.at[group], normed.at[group], 2, group_peer(k)))

    wait_all(ids, groups - 1, recv_sem.at[0])
    row_iota = lax.broadcasted_iota(jnp.int32, (rows, row_group), 0)
    lane_iota = lax.broadcasted_iota(jnp.int32, (rows, row_group), 1)
    dealt = jnp.zeros((rows, row_group), jnp.float32)
    owned = jnp.zeros((rows, row_group), jnp.float32)
    for k in range(groups):
        slots = ids[k, 0:1, 0:row_group]
        wanted = ids[k, 1:2, 0:row_group].astype(jnp.float32)
        dealt = dealt + jnp.where(row_iota == slots, wanted, 0.0)
        owned = owned + jnp.where(row_iota == lane_iota + k * row_group, wanted, 0.0)
    offset = me * vocab_dev
    vocab_iota = lax.broadcasted_iota(jnp.int32, (rows, vocab_dev), 1) + offset
    dealt_ids = jnp.sum(dealt, axis=1, keepdims=True).astype(jnp.int32)
    owned_ids = jnp.sum(owned, axis=1, keepdims=True).astype(jnp.int32)
    one_hot = jnp.where(dealt_ids == vocab_iota, 1.0, 0.0).astype(jnp.bfloat16)
    head_copy.wait()
    picked[...] = jnp.dot(one_hot, head[...], preferred_element_type=jnp.float32)
    for k in range(groups):
        picked_out[k] = picked[k * row_group : (k + 1) * row_group, :].astype(jnp.bfloat16)

    def columns(v):
        return pl.ds(pl.multiple_of(lax.div(v * tiles, shards) * LANES, LANES), span)

    def send_piece(k):
        peer = lax.rem(me + k, devices)
        peer_group, peer_shard = lax.div(peer, shards), lax.rem(peer, shards)
        send(picked_out.at[peer_group, :, columns(peer_shard)], picked_in.at[me], 3, (peer_group, peer_shard))

    each(1, devices, send_piece)
    picked_in[me] = picked_out[group, :, columns(shard)]

    wait_all(normed, groups - 1, recv_sem.at[2])
    for k in range(groups):
        rows_all[k * row_group : (k + 1) * row_group, :] = normed[k].astype(jnp.float32)
    logits = lax.dot_general(
        rows_all[...].astype(jnp.bfloat16),
        head[...],
        (((1,), (1,)), ((), ())),
        preferred_element_type=jnp.float32,
    )
    top = jnp.max(logits, axis=1, keepdims=True)
    shifted = logits - top
    expons = jnp.exp(shifted)
    columns_of = (
        top,
        jnp.sum(expons, axis=1, keepdims=True),
        jnp.sum(expons * shifted, axis=1, keepdims=True),
        jnp.sum(jnp.where(owned_ids == vocab_iota, logits, 0.0), axis=1, keepdims=True),
    )
    lanes = stats_one.shape[2]
    diagonal = lax.broadcasted_iota(jnp.int32, (rows, lanes), 0) == lax.broadcasted_iota(
        jnp.int32, (rows, lanes), 1
    )
    put_stats(
        stats_one,
        shard,
        [jnp.sum(jnp.where(diagonal, column, 0.0), axis=0, keepdims=True) for column in columns_of],
    )
    each(1, shards, lambda k: send(stats_one.at[shard], stats_one.at[shard], 4, shard_peer(k)))

    wait_all(picked_in, devices - 1, recv_sem.at[3])
    if devices <= UNROLL_MAX:
        total = jnp.sum(picked_in[...].astype(jnp.float32), axis=0)
    else:
        total = lax.fori_loop(
            0,
            devices,
            lambda k, so_far: so_far + picked_in[k].astype(jnp.float32),
            jnp.zeros((row_group, span), jnp.float32),
        )
    summed[shard] = total.astype(jnp.bfloat16)
    each(1, shards, lambda k: send(summed.at[shard], summed.at[shard], 5, shard_peer(k)))

    wait_all(stats_one, shards - 1, recv_sem.at[4])
    put_stats(stats_two, group, merged(stats_one))
    each(1, groups, lambda k: send(stats_two.at[group], stats_two.at[group], 6, group_peer(k)))

    qkv_copy.wait()
    wait_all(summed, shards - 1, recv_sem.at[5])
    for v in range(shards):
        embedded[:, starts[v] * LANES : starts[v] * LANES + span] = summed[v].astype(jnp.float32)
    first_normed = rms_scaled(embedded[...], first_gain_ref[...])
    out_ref[...] = jnp.dot(first_normed, qkv[...], preferred_element_type=jnp.float32).astype(out_ref.dtype)

    wait_all(stats_two, groups - 1, recv_sem.at[6])
    row_top, row_total, row_weighted, row_target = merged(stats_two)
    log_total = jnp.log(row_total)
    logprob = row_target - row_top - log_total
    entropy = log_total - row_weighted / row_total
    for ref, values in ((logprob_ref, logprob), (entropy_ref, entropy)):
        mine = values[:, 0:row_group]
        for k in range(1, groups):
            mine = jnp.where(group == k, values[:, k * row_group : (k + 1) * row_group], mine)
        ref[...] = mine

    wait_all(ids, groups - 1, send_sem.at[0])
    wait_all(pieces, shards - 1, send_sem.at[1])
    wait_all(normed, groups - 1, send_sem.at[2])
    wait_all(picked_in, devices - 1, send_sem.at[3])
    wait_all(stats_one, shards - 1, send_sem.at[4])
    wait_all(summed, shards - 1, send_sem.at[5])
    wait_all(stats_two, groups - 1, send_sem.at[6])


def local(groups, shards, hidden, dealt_slot, targets, final_gain, vocab_head, first_gain, qkv_weight):
    row_group, cols = hidden.shape
    rows = row_group * groups
    width_all = vocab_head.shape[1]
    tiles = width_all // LANES
    starts = [v * tiles // shards for v in range(shards)]
    width = max(b - a for a, b in zip(starts, starts[1:] + [tiles]))
    span = width * LANES
    lanes = -(-rows // LANES) * LANES
    qkv_cols = qkv_weight.shape[1]
    vmem = pl.BlockSpec(memory_space=pltpu.VMEM)
    hbm = pl.BlockSpec(memory_space=pl.ANY)
    logprob, entropy, projected = pl.pallas_call(
        functools.partial(kernel, groups, shards, starts, width),
        out_shape=(
            jax.ShapeDtypeStruct((1, row_group), jnp.float32),
            jax.ShapeDtypeStruct((1, row_group), jnp.float32),
            jax.ShapeDtypeStruct((row_group, qkv_cols), jnp.bfloat16),
        ),
        in_specs=[vmem, vmem, vmem, vmem, hbm, vmem, hbm],
        out_specs=(vmem, vmem, vmem),
        scratch_shapes=[
            pltpu.VMEM(vocab_head.shape, jnp.bfloat16),
            pltpu.VMEM(qkv_weight.shape, jnp.bfloat16),
            pltpu.VMEM((groups, 8, LANES), jnp.int32),
            pltpu.VMEM((shards, row_group, cols), jnp.bfloat16),
            pltpu.VMEM((row_group, width_all), jnp.float32),
            pltpu.VMEM((groups, row_group, width_all), jnp.bfloat16),
            pltpu.VMEM((rows, width_all), jnp.float32),
            pltpu.VMEM((rows, width_all), jnp.float32),
            pltpu.VMEM((groups, row_group, width_all), jnp.bfloat16),
            pltpu.VMEM((groups * shards, row_group, span), jnp.bfloat16),
            pltpu.VMEM((shards, row_group, span), jnp.bfloat16),
            pltpu.VMEM((row_group, width_all), jnp.float32),
            pltpu.VMEM((shards, 8, lanes), jnp.float32),
            pltpu.VMEM((groups, 8, lanes), jnp.float32),
            pltpu.SemaphoreType.DMA((2,)),
            pltpu.SemaphoreType.DMA((7,)),
            pltpu.SemaphoreType.DMA((7,)),
        ],
        compiler_params=pltpu.CompilerParams(
            collective_id=0, has_side_effects=True, vmem_limit_bytes=48 * 1024 * 1024
        ),
    )(
        hidden,
        dealt_slot.reshape(1, row_group),
        targets.reshape(1, row_group),
        final_gain.reshape(1, width_all),
        vocab_head,
        first_gain.reshape(1, width_all),
        qkv_weight,
    )
    return (logprob.reshape(row_group), entropy.reshape(row_group), projected.T)


def solution(mesh):
    return jax.shard_map(
        functools.partial(local, mesh.shape["group"], mesh.shape["vocab"]),
        mesh=mesh,
        in_specs=(
            P("group", "vocab"),
            P("group"),
            P("group"),
            P(),
            P(("group", "vocab"), None),
            P(),
            P(None, "vocab"),
        ),
        out_specs=(P("group"), P("group"), P("vocab", "group")),
        check_vma=False,
    )
```

```python
import functools

import jax
import jax.numpy as jnp
from jax import lax
from jax.experimental import pallas as pl
from jax.experimental.pallas import tpu as pltpu
from jax.sharding import PartitionSpec as P

eps = 1e-06
MESH = pl.DeviceIdType.MESH
LANES = 128
UNROLL_MAX = 32


def each(first, last, body):
    if last - first <= UNROLL_MAX:
        for k in range(first, last):
            body(k)
    else:

        def step(k, carry):
            body(k)
            return carry

        lax.fori_loop(first, last, step, 0)


def rms_scaled(wide, gain):
    factor = lax.rsqrt(jnp.mean(wide * wide, axis=-1, keepdims=True) + eps)
    return (wide * factor * gain).astype(jnp.bfloat16)


def merged(ref):
    tops = ref[:, 0:1, :]
    totals = ref[:, 1:2, :]
    top = jnp.max(tops, axis=0, keepdims=True)
    gap = tops - top
    scale = jnp.exp(gap)
    total = jnp.sum(scale * totals, axis=0)
    weighted = jnp.sum(scale * (ref[:, 2:3, :] + totals * gap), axis=0)
    target = jnp.sum(ref[:, 3:4, :], axis=0)
    return top[0], total, weighted, target


def put_stats(ref, k, stats):
    for row, stat in enumerate(stats):
        ref[k, row : row + 1, :] = stat


def kernel(
    groups,
    shards,
    starts,
    width,
    hidden_hbm,
    slot_hbm,
    target_hbm,
    final_gain_hbm,
    head_hbm,
    first_gain_hbm,
    qkv_hbm,
    logprob_ref,
    entropy_ref,
    out_ref,
    head,
    qkv,
    slot_ref,
    target_ref,
    final_gain_ref,
    first_gain_ref,
    ids,
    pieces,
    wide_rows,
    normed,
    rows_all,
    picked,
    picked_out,
    picked_in,
    summed,
    embedded,
    stats_one,
    stats_two,
    local_sem,
    send_sem,
    recv_sem,
):
    group = lax.axis_index("group")
    shard = lax.axis_index("vocab")
    row_group, cols = hidden_hbm.shape
    rows = row_group * groups
    vocab_dev, width_all = head.shape
    tiles = width_all // LANES
    devices = groups * shards
    me = group * shards + shard
    span = width * LANES

    def group_peer(k):
        return (lax.rem(group + k, groups), shard)

    def shard_peer(k):
        return (group, lax.rem(shard + k, shards))

    def send(src, dst, phase, peer):
        pltpu.make_async_remote_copy(
            src_ref=src,
            dst_ref=dst,
            send_sem=send_sem.at[phase],
            recv_sem=recv_sem.at[phase],
            device_id=peer,
            device_id_type=MESH,
        ).start()

    def wait_all(ref, count, sem):
        if count > 0:
            part = ref.at[pl.ds(0, count)]
            pltpu.make_async_copy(part, part, sem).wait()

    barrier = pltpu.get_barrier_semaphore()
    each(1, groups, lambda k: pl.semaphore_signal(barrier, inc=1, device_id=group_peer(k), device_id_type=MESH))
    each(1, shards, lambda k: pl.semaphore_signal(barrier, inc=1, device_id=shard_peer(k), device_id_type=MESH))
    slot_copy = pltpu.make_async_copy(slot_hbm, slot_ref, local_sem.at[0])
    target_copy = pltpu.make_async_copy(target_hbm, target_ref, local_sem.at[1])
    hidden_copy = pltpu.make_async_copy(hidden_hbm, pieces.at[shard], local_sem.at[2])
    final_copy = pltpu.make_async_copy(final_gain_hbm, final_gain_ref, local_sem.at[3])
    head_copy = pltpu.make_async_copy(head_hbm, head, local_sem.at[4])
    first_copy = pltpu.make_async_copy(first_gain_hbm, first_gain_ref, local_sem.at[5])
    qkv_copy = pltpu.make_async_copy(qkv_hbm, qkv, local_sem.at[6])
    for copy in (slot_copy, target_copy, hidden_copy, final_copy, head_copy, first_copy, qkv_copy):
        copy.start()
    slot_copy.wait()
    target_copy.wait()
    ids[group, 0:1, 0:row_group] = slot_ref[...]
    ids[group, 1:2, 0:row_group] = target_ref[...]
    hidden_copy.wait()
    pl.semaphore_wait(barrier, groups + shards - 2)

    each(1, groups, lambda k: send(ids.at[group], ids.at[group], 0, group_peer(k)))
    each(1, shards, lambda k: send(pieces.at[shard], pieces.at[shard], 1, shard_peer(k)))

    wait_all(pieces, shards - 1, recv_sem.at[1])
    for v in range(shards):
        wide_rows[:, v * cols : (v + 1) * cols] = pieces[v].astype(jnp.float32)
    final_copy.wait()
    normed[group] = rms_scaled(wide_rows[...], final_gain_ref[...])
    each(1, groups, lambda k: send(normed.at[group], normed.at[group], 2, group_peer(k)))

    wait_all(ids, groups - 1, recv_sem.at[0])
    row_iota = lax.broadcasted_iota(jnp.int32, (rows, row_group), 0)
    lane_iota = lax.broadcasted_iota(jnp.int32, (rows, row_group), 1)
    dealt = jnp.zeros((rows, row_group), jnp.float32)
    owned = jnp.zeros((rows, row_group), jnp.float32)
    for k in range(groups):
        slots = ids[k, 0:1, 0:row_group]
        wanted = ids[k, 1:2, 0:row_group].astype(jnp.float32)
        dealt = dealt + jnp.where(row_iota == slots, wanted, 0.0)
        owned = owned + jnp.where(row_iota == lane_iota + k * row_group, wanted, 0.0)
    offset = me * vocab_dev
    vocab_iota = lax.broadcasted_iota(jnp.int32, (rows, vocab_dev), 1) + offset
    dealt_ids = jnp.sum(dealt, axis=1, keepdims=True).astype(jnp.int32)
    owned_ids = jnp.sum(owned, axis=1, keepdims=True).astype(jnp.int32)
    one_hot = jnp.where(dealt_ids == vocab_iota, 1.0, 0.0).astype(jnp.bfloat16)
    head_copy.wait()
    picked[...] = jnp.dot(one_hot, head[...], preferred_element_type=jnp.float32)
    for k in range(groups):
        picked_out[k] = picked[k * row_group : (k + 1) * row_group, :].astype(jnp.bfloat16)

    def columns(v):
        return pl.ds(pl.multiple_of(lax.div(v * tiles, shards) * LANES, LANES), span)

    def send_piece(k):
        peer = lax.rem(me + k, devices)
        peer_group, peer_shard = lax.div(peer, shards), lax.rem(peer, shards)
        send(picked_out.at[peer_group, :, columns(peer_shard)], picked_in.at[me], 3, (peer_group, peer_shard))

    each(1, devices, send_piece)
    picked_in[me] = picked_out[group, :, columns(shard)]

    wait_all(normed, groups - 1, recv_sem.at[2])
    for k in range(groups):
        rows_all[k * row_group : (k + 1) * row_group, :] = normed[k].astype(jnp.float32)
    logits = lax.dot_general(
        rows_all[...].astype(jnp.bfloat16),
        head[...],
        (((1,), (1,)), ((), ())),
        preferred_element_type=jnp.float32,
    )
    top = jnp.max(logits, axis=1, keepdims=True)
    shifted = logits - top
    expons = jnp.exp(shifted)
    columns_of = (
        top,
        jnp.sum(expons, axis=1, keepdims=True),
        jnp.sum(expons * shifted, axis=1, keepdims=True),
        jnp.sum(jnp.where(owned_ids == vocab_iota, logits, 0.0), axis=1, keepdims=True),
    )
    lanes = stats_one.shape[2]
    diagonal = lax.broadcasted_iota(jnp.int32, (rows, lanes), 0) == lax.broadcasted_iota(
        jnp.int32, (rows, lanes), 1
    )
    put_stats(
        stats_one,
        shard,
        [jnp.sum(jnp.where(diagonal, column, 0.0), axis=0, keepdims=True) for column in columns_of],
    )
    each(1, shards, lambda k: send(stats_one.at[shard], stats_one.at[shard], 4, shard_peer(k)))

    wait_all(picked_in, devices - 1, recv_sem.at[3])
    if devices <= UNROLL_MAX:
        total = jnp.sum(picked_in[...].astype(jnp.float32), axis=0)
    else:
        total = lax.fori_loop(
            0,
            devices,
            lambda k, so_far: so_far + picked_in[k].astype(jnp.float32),
            jnp.zeros((row_group, span), jnp.float32),
        )
    summed[shard] = total.astype(jnp.bfloat16)
    each(1, shards, lambda k: send(summed.at[shard], summed.at[shard], 5, shard_peer(k)))

    wait_all(stats_one, shards - 1, recv_sem.at[4])
    put_stats(stats_two, group, merged(stats_one))
    each(1, groups, lambda k: send(stats_two.at[group], stats_two.at[group], 6, group_peer(k)))

    first_copy.wait()
    qkv_copy.wait()
    wait_all(summed, shards - 1, recv_sem.at[5])
    for v in range(shards):
        embedded[:, starts[v] * LANES : starts[v] * LANES + span] = summed[v].astype(jnp.float32)
    first_normed = rms_scaled(embedded[...], first_gain_ref[...])
    out_ref[...] = jnp.dot(first_normed, qkv[...], preferred_element_type=jnp.float32).astype(out_ref.dtype)

    wait_all(stats_two, groups - 1, recv_sem.at[6])
    row_top, row_total, row_weighted, row_target = merged(stats_two)
    log_total = jnp.log(row_total)
    logprob = row_target - row_top - log_total
    entropy = log_total - row_weighted / row_total
    for ref, values in ((logprob_ref, logprob), (entropy_ref, entropy)):
        mine = values[:, 0:row_group]
        for k in range(1, groups):
            mine = jnp.where(group == k, values[:, k * row_group : (k + 1) * row_group], mine)
        ref[...] = mine

    wait_all(ids, groups - 1, send_sem.at[0])
    wait_all(pieces, shards - 1, send_sem.at[1])
    wait_all(normed, groups - 1, send_sem.at[2])
    wait_all(picked_in, devices - 1, send_sem.at[3])
    wait_all(stats_one, shards - 1, send_sem.at[4])
    wait_all(summed, shards - 1, send_sem.at[5])
    wait_all(stats_two, groups - 1, send_sem.at[6])


def local(groups, shards, hidden, dealt_slot, targets, final_gain, vocab_head, first_gain, qkv_weight):
    row_group, cols = hidden.shape
    rows = row_group * groups
    width_all = vocab_head.shape[1]
    tiles = width_all // LANES
    starts = [v * tiles // shards for v in range(shards)]
    width = max(b - a for a, b in zip(starts, starts[1:] + [tiles]))
    span = width * LANES
    lanes = -(-rows // LANES) * LANES
    qkv_cols = qkv_weight.shape[1]
    vmem = pl.BlockSpec(memory_space=pltpu.VMEM)
    hbm = pl.BlockSpec(memory_space=pltpu.HBM)
    logprob, entropy, projected = pl.pallas_call(
        functools.partial(kernel, groups, shards, starts, width),
        out_shape=(
            jax.ShapeDtypeStruct((1, row_group), jnp.float32),
            jax.ShapeDtypeStruct((1, row_group), jnp.float32),
            jax.ShapeDtypeStruct((row_group, qkv_cols), jnp.bfloat16),
        ),
        in_specs=[hbm] * 7,
        out_specs=(vmem, vmem, vmem),
        scratch_shapes=[
            pltpu.VMEM(vocab_head.shape, jnp.bfloat16),
            pltpu.VMEM(qkv_weight.shape, jnp.bfloat16),
            pltpu.VMEM((1, row_group), jnp.int32),
            pltpu.VMEM((1, row_group), jnp.int32),
            pltpu.VMEM((1, width_all), jnp.float32),
            pltpu.VMEM((1, width_all), jnp.float32),
            pltpu.VMEM((groups, 8, LANES), jnp.int32),
            pltpu.VMEM((shards, row_group, cols), jnp.bfloat16),
            pltpu.VMEM((row_group, width_all), jnp.float32),
            pltpu.VMEM((groups, row_group, width_all), jnp.bfloat16),
            pltpu.VMEM((rows, width_all), jnp.float32),
            pltpu.VMEM((rows, width_all), jnp.float32),
            pltpu.VMEM((groups, row_group, width_all), jnp.bfloat16),
            pltpu.VMEM((groups * shards, row_group, span), jnp.bfloat16),
            pltpu.VMEM((shards, row_group, span), jnp.bfloat16),
            pltpu.VMEM((row_group, width_all), jnp.float32),
            pltpu.VMEM((shards, 8, lanes), jnp.float32),
            pltpu.VMEM((groups, 8, lanes), jnp.float32),
            pltpu.SemaphoreType.DMA((7,)),
            pltpu.SemaphoreType.DMA((7,)),
            pltpu.SemaphoreType.DMA((7,)),
        ],
        compiler_params=pltpu.CompilerParams(
            collective_id=0, has_side_effects=True, vmem_limit_bytes=63 * 1024 * 1024
        ),
    )(
        hidden,
        dealt_slot.reshape(1, row_group),
        targets.reshape(1, row_group),
        final_gain.reshape(1, width_all),
        vocab_head,
        first_gain.reshape(1, width_all),
        qkv_weight,
    )
    return (logprob.reshape(row_group), entropy.reshape(row_group), projected.T)


def solution(mesh):
    return jax.shard_map(
        functools.partial(local, mesh.shape["group"], mesh.shape["vocab"]),
        mesh=mesh,
        in_specs=(
            P("group", "vocab"),
            P("group"),
            P("group"),
            P(),
            P(("group", "vocab"), None),
            P(),
            P(None, "vocab"),
        ),
        out_specs=(P("group"), P("group"), P("vocab", "group")),
        check_vma=False,
    )
```

```python
import functools

import jax
import jax.numpy as jnp
from jax import lax
from jax.experimental import pallas as pl
from jax.experimental.pallas import tpu as pltpu
from jax.sharding import PartitionSpec as P

eps = 1e-06
MESH = pl.DeviceIdType.MESH
LANES = 128
UNROLL_MAX = 32


def each(first, last, body):
    if last - first <= UNROLL_MAX:
        for k in range(first, last):
            body(k)
    else:

        def step(k, carry):
            body(k)
            return carry

        lax.fori_loop(first, last, step, 0)


def rms_scaled(wide, gain):
    factor = lax.rsqrt(jnp.mean(wide * wide, axis=-1, keepdims=True) + eps)
    return (wide * factor * gain).astype(jnp.bfloat16)


def merged(ref):
    tops = ref[:, 0:1, :]
    totals = ref[:, 1:2, :]
    top = jnp.max(tops, axis=0, keepdims=True)
    gap = tops - top
    scale = jnp.exp(gap)
    total = jnp.sum(scale * totals, axis=0)
    weighted = jnp.sum(scale * (ref[:, 2:3, :] + totals * gap), axis=0)
    target = jnp.sum(ref[:, 3:4, :], axis=0)
    return top[0], total, weighted, target


def put_stats(ref, k, stats):
    for row, stat in enumerate(stats):
        ref[k, row : row + 1, :] = stat


def kernel(
    groups,
    shards,
    starts,
    width,
    hidden_hbm,
    slot_hbm,
    target_hbm,
    final_gain_hbm,
    head_hbm,
    first_gain_hbm,
    qkv_hbm,
    logprob_ref,
    entropy_ref,
    out_ref,
    head,
    qkv,
    slot_ref,
    target_ref,
    final_gain_ref,
    first_gain_ref,
    ids,
    pieces,
    wide_rows,
    normed,
    rows_all,
    picked,
    picked_out,
    picked_in,
    summed,
    embedded,
    stats_one,
    stats_two,
    local_sem,
    send_sem,
    recv_sem,
):
    group = lax.axis_index("group")
    shard = lax.axis_index("vocab")
    row_group, cols = hidden_hbm.shape
    rows = row_group * groups
    vocab_dev, width_all = head.shape
    tiles = width_all // LANES
    devices = groups * shards
    me = group * shards + shard
    span = width * LANES

    def group_peer(k):
        return (lax.rem(group + k, groups), shard)

    def shard_peer(k):
        return (group, lax.rem(shard + k, shards))

    def send(src, dst, phase, peer):
        pltpu.make_async_remote_copy(
            src_ref=src,
            dst_ref=dst,
            send_sem=send_sem.at[phase],
            recv_sem=recv_sem.at[phase],
            device_id=peer,
            device_id_type=MESH,
        ).start()

    def wait_all(ref, count, sem):
        if count > 0:
            part = ref.at[pl.ds(0, count)]
            pltpu.make_async_copy(part, part, sem).wait()

    barrier = pltpu.get_barrier_semaphore()
    each(1, groups, lambda k: pl.semaphore_signal(barrier, inc=1, device_id=group_peer(k), device_id_type=MESH))
    each(1, shards, lambda k: pl.semaphore_signal(barrier, inc=1, device_id=shard_peer(k), device_id_type=MESH))
    slot_copy = pltpu.make_async_copy(slot_hbm, slot_ref, local_sem.at[0])
    target_copy = pltpu.make_async_copy(target_hbm, target_ref, local_sem.at[1])
    hidden_copy = pltpu.make_async_copy(hidden_hbm, pieces.at[shard], local_sem.at[2])
    final_copy = pltpu.make_async_copy(final_gain_hbm, final_gain_ref.at[0], local_sem.at[3])
    head_copy = pltpu.make_async_copy(head_hbm, head, local_sem.at[4])
    first_copy = pltpu.make_async_copy(first_gain_hbm, first_gain_ref.at[0], local_sem.at[5])
    qkv_copy = pltpu.make_async_copy(qkv_hbm, qkv, local_sem.at[6])
    for copy in (slot_copy, target_copy, hidden_copy, final_copy, head_copy, first_copy, qkv_copy):
        copy.start()
    slot_copy.wait()
    target_copy.wait()
    ids[group, 0:1, 0:row_group] = slot_ref[...]
    ids[group, 1:2, 0:row_group] = target_ref[...]
    hidden_copy.wait()
    pl.semaphore_wait(barrier, groups + shards - 2)

    each(1, groups, lambda k: send(ids.at[group], ids.at[group], 0, group_peer(k)))
    each(1, shards, lambda k: send(pieces.at[shard], pieces.at[shard], 1, shard_peer(k)))

    wait_all(ids, groups - 1, recv_sem.at[0])
    row_iota = lax.broadcasted_iota(jnp.int32, (rows, row_group), 0)
    lane_iota = lax.broadcasted_iota(jnp.int32, (rows, row_group), 1)
    dealt = jnp.zeros((rows, row_group), jnp.float32)
    owned = jnp.zeros((rows, row_group), jnp.float32)
    for k in range(groups):
        slots = ids[k, 0:1, 0:row_group]
        wanted = ids[k, 1:2, 0:row_group].astype(jnp.float32)
        dealt = dealt + jnp.where(row_iota == slots, wanted, 0.0)
        owned = owned + jnp.where(row_iota == lane_iota + k * row_group, wanted, 0.0)
    offset = me * vocab_dev
    vocab_iota = lax.broadcasted_iota(jnp.int32, (rows, vocab_dev), 1) + offset
    dealt_ids = jnp.sum(dealt, axis=1, keepdims=True).astype(jnp.int32)
    owned_ids = jnp.sum(owned, axis=1, keepdims=True).astype(jnp.int32)
    one_hot = jnp.where(dealt_ids == vocab_iota, 1.0, 0.0).astype(jnp.bfloat16)
    head_copy.wait()
    picked[...] = jnp.dot(one_hot, head[...], preferred_element_type=jnp.float32)
    for k in range(groups):
        picked_out[k] = picked[k * row_group : (k + 1) * row_group, :].astype(jnp.bfloat16)

    def columns(v):
        return pl.ds(pl.multiple_of(lax.div(v * tiles, shards) * LANES, LANES), span)

    def send_piece(k):
        peer = lax.rem(me + k, devices)
        peer_group, peer_shard = lax.div(peer, shards), lax.rem(peer, shards)
        send(picked_out.at[peer_group, :, columns(peer_shard)], picked_in.at[me], 3, (peer_group, peer_shard))

    each(1, devices, send_piece)
    picked_in[me] = picked_out[group, :, columns(shard)]

    wait_all(pieces, shards - 1, recv_sem.at[1])
    for v in range(shards):
        wide_rows[:, v * cols : (v + 1) * cols] = pieces[v].astype(jnp.float32)
    final_copy.wait()
    normed[group] = rms_scaled(wide_rows[...], final_gain_ref[...])
    each(1, groups, lambda k: send(normed.at[group], normed.at[group], 2, group_peer(k)))

    wait_all(normed, groups - 1, recv_sem.at[2])
    for k in range(groups):
        rows_all[k * row_group : (k + 1) * row_group, :] = normed[k].astype(jnp.float32)
    logits = lax.dot_general(
        rows_all[...].astype(jnp.bfloat16),
        head[...],
        (((1,), (1,)), ((), ())),
        preferred_element_type=jnp.float32,
    )
    top = jnp.max(logits, axis=1, keepdims=True)
    shifted = logits - top
    expons = jnp.exp(shifted)
    columns_of = (
        top,
        jnp.sum(expons, axis=1, keepdims=True),
        jnp.sum(expons * shifted, axis=1, keepdims=True),
        jnp.sum(jnp.where(owned_ids == vocab_iota, logits, 0.0), axis=1, keepdims=True),
    )
    lanes = stats_one.shape[2]
    diagonal = lax.broadcasted_iota(jnp.int32, (rows, lanes), 0) == lax.broadcasted_iota(
        jnp.int32, (rows, lanes), 1
    )
    put_stats(
        stats_one,
        shard,
        [jnp.sum(jnp.where(diagonal, column, 0.0), axis=0, keepdims=True) for column in columns_of],
    )
    each(1, shards, lambda k: send(stats_one.at[shard], stats_one.at[shard], 4, shard_peer(k)))

    wait_all(picked_in, devices - 1, recv_sem.at[3])
    if devices <= UNROLL_MAX:
        total = jnp.sum(picked_in[...].astype(jnp.float32), axis=0)
    else:
        total = lax.fori_loop(
            0,
            devices,
            lambda k, so_far: so_far + picked_in[k].astype(jnp.float32),
            jnp.zeros((row_group, span), jnp.float32),
        )
    summed[shard] = total.astype(jnp.bfloat16)
    each(1, shards, lambda k: send(summed.at[shard], summed.at[shard], 5, shard_peer(k)))

    wait_all(stats_one, shards - 1, recv_sem.at[4])
    put_stats(stats_two, group, merged(stats_one))
    each(1, groups, lambda k: send(stats_two.at[group], stats_two.at[group], 6, group_peer(k)))

    first_copy.wait()
    qkv_copy.wait()
    wait_all(summed, shards - 1, recv_sem.at[5])
    for v in range(shards):
        embedded[:, starts[v] * LANES : starts[v] * LANES + span] = summed[v].astype(jnp.float32)
    first_normed = rms_scaled(embedded[...], first_gain_ref[...])
    out_ref[...] = jnp.dot(first_normed, qkv[...], preferred_element_type=jnp.float32).astype(out_ref.dtype)

    wait_all(stats_two, groups - 1, recv_sem.at[6])
    row_top, row_total, row_weighted, row_target = merged(stats_two)
    log_total = jnp.log(row_total)
    logprob = row_target - row_top - log_total
    entropy = log_total - row_weighted / row_total
    for ref, values in ((logprob_ref, logprob), (entropy_ref, entropy)):
        mine = values[:, 0:row_group]
        for k in range(1, groups):
            mine = jnp.where(group == k, values[:, k * row_group : (k + 1) * row_group], mine)
        ref[...] = mine

    wait_all(ids, groups - 1, send_sem.at[0])
    wait_all(pieces, shards - 1, send_sem.at[1])
    wait_all(normed, groups - 1, send_sem.at[2])
    wait_all(picked_in, devices - 1, send_sem.at[3])
    wait_all(stats_one, shards - 1, send_sem.at[4])
    wait_all(summed, shards - 1, send_sem.at[5])
    wait_all(stats_two, groups - 1, send_sem.at[6])


def hand_over(*refs):
    sems = refs[-1]
    copies = [pltpu.make_async_copy(refs[k], refs[k + 3], sems.at[k]) for k in range(3)]
    for copy in copies:
        copy.start()
    for copy in copies:
        copy.wait()


def local(groups, shards, hidden, dealt_slot, targets, final_gain, vocab_head, first_gain, qkv_weight):
    row_group, cols = hidden.shape
    rows = row_group * groups
    width_all = vocab_head.shape[1]
    tiles = width_all // LANES
    starts = [v * tiles // shards for v in range(shards)]
    width = max(b - a for a, b in zip(starts, starts[1:] + [tiles]))
    span = width * LANES
    lanes = -(-rows // LANES) * LANES
    qkv_cols = qkv_weight.shape[1]
    vmem = pl.BlockSpec(memory_space=pltpu.VMEM)
    hbm = pl.BlockSpec(memory_space=pltpu.HBM)
    logprob, entropy, projected = pl.pallas_call(
        functools.partial(kernel, groups, shards, starts, width),
        out_shape=(
            jax.ShapeDtypeStruct((1, row_group), jnp.float32),
            jax.ShapeDtypeStruct((1, row_group), jnp.float32),
            jax.ShapeDtypeStruct((row_group, qkv_cols), jnp.bfloat16),
        ),
        in_specs=[hbm] * 7,
        out_specs=(vmem, vmem, vmem),
        scratch_shapes=[
            pltpu.VMEM(vocab_head.shape, jnp.bfloat16),
            pltpu.VMEM(qkv_weight.shape, jnp.bfloat16),
            pltpu.VMEM((1, row_group), jnp.int32),
            pltpu.VMEM((1, row_group), jnp.int32),
            pltpu.VMEM((1, width_all), jnp.float32),
            pltpu.VMEM((1, width_all), jnp.float32),
            pltpu.VMEM((groups, 8, LANES), jnp.int32),
            pltpu.VMEM((shards, row_group, cols), jnp.bfloat16),
            pltpu.VMEM((row_group, width_all), jnp.float32),
            pltpu.VMEM((groups, row_group, width_all), jnp.bfloat16),
            pltpu.VMEM((rows, width_all), jnp.float32),
            pltpu.VMEM((rows, width_all), jnp.float32),
            pltpu.VMEM((groups, row_group, width_all), jnp.bfloat16),
            pltpu.VMEM((groups * shards, row_group, span), jnp.bfloat16),
            pltpu.VMEM((shards, row_group, span), jnp.bfloat16),
            pltpu.VMEM((row_group, width_all), jnp.float32),
            pltpu.VMEM((shards, 8, lanes), jnp.float32),
            pltpu.VMEM((groups, 8, lanes), jnp.float32),
            pltpu.SemaphoreType.DMA((7,)),
            pltpu.SemaphoreType.DMA((7,)),
            pltpu.SemaphoreType.DMA((7,)),
        ],
        compiler_params=pltpu.CompilerParams(
            collective_id=0, has_side_effects=True, vmem_limit_bytes=63 * 1024 * 1024
        ),
    )(
        hidden,
        dealt_slot.reshape(1, row_group),
        targets.reshape(1, row_group),
        final_gain,
        vocab_head,
        first_gain,
        qkv_weight,
    )
    results = (logprob.reshape(row_group), entropy.reshape(row_group), projected)
    logprob, entropy, projected = pl.pallas_call(
        hand_over,
        out_shape=tuple(jax.ShapeDtypeStruct(r.shape, r.dtype) for r in results),
        in_specs=[hbm] * 3,
        out_specs=(hbm,) * 3,
        scratch_shapes=[pltpu.SemaphoreType.DMA((3,))],
    )(*results)
    return (logprob, entropy, projected.T)


def solution(mesh):
    return jax.shard_map(
        functools.partial(local, mesh.shape["group"], mesh.shape["vocab"]),
        mesh=mesh,
        in_specs=(
            P("group", "vocab"),
            P("group"),
            P("group"),
            P(),
            P(("group", "vocab"), None),
            P(),
            P(None, "vocab"),
        ),
        out_specs=(P("group"), P("group"), P("vocab", "group")),
        check_vma=False,
    )
```

```python
import functools

import jax
import jax.numpy as jnp
from jax import lax
from jax.experimental import pallas as pl
from jax.experimental.pallas import tpu as pltpu
from jax.sharding import PartitionSpec as P

eps = 1e-06
MESH = pl.DeviceIdType.MESH
LANES = 128
UNROLL_MAX = 32


def each(first, last, body):
    if last - first <= UNROLL_MAX:
        for k in range(first, last):
            body(k)
    else:

        def step(k, carry):
            body(k)
            return carry

        lax.fori_loop(first, last, step, 0)


def rms_scaled(wide, gain):
    factor = lax.rsqrt(jnp.mean(wide * wide, axis=-1, keepdims=True) + eps)
    return (wide * factor * gain).astype(jnp.bfloat16)


def merged(ref):
    tops = ref[:, 0:1, :]
    totals = ref[:, 1:2, :]
    top = jnp.max(tops, axis=0, keepdims=True)
    gap = tops - top
    scale = jnp.exp(gap)
    total = jnp.sum(scale * totals, axis=0)
    weighted = jnp.sum(scale * (ref[:, 2:3, :] + totals * gap), axis=0)
    target = jnp.sum(ref[:, 3:4, :], axis=0)
    return top[0], total, weighted, target


def put_stats(ref, k, stats):
    for row, stat in enumerate(stats):
        ref[k, row : row + 1, :] = stat


def kernel(
    groups,
    shards,
    starts,
    width,
    hidden_hbm,
    slot_hbm,
    target_hbm,
    final_gain_hbm,
    head_hbm,
    first_gain_hbm,
    qkv_hbm,
    logprob_ref,
    entropy_ref,
    out_ref,
    head,
    qkv,
    slot_ref,
    target_ref,
    final_gain_ref,
    first_gain_ref,
    ids,
    pieces,
    rows_all,
    picked,
    picked_out,
    picked_in,
    summed,
    embedded,
    stats,
    local_sem,
    send_sem,
    recv_sem,
):
    group = lax.axis_index("group")
    shard = lax.axis_index("vocab")
    row_group, cols = hidden_hbm.shape
    rows = row_group * groups
    vocab_dev, width_all = head.shape
    tiles = width_all // LANES
    devices = groups * shards
    me = group * shards + shard
    span = width * LANES

    def group_peer(k):
        return (lax.rem(group + k, groups), shard)

    def any_peer(k):
        peer = lax.rem(me + k, devices)
        return (lax.div(peer, shards), lax.rem(peer, shards))

    def shard_peer(k):
        return (group, lax.rem(shard + k, shards))

    def send(src, dst, phase, peer):
        pltpu.make_async_remote_copy(
            src_ref=src,
            dst_ref=dst,
            send_sem=send_sem.at[phase],
            recv_sem=recv_sem.at[phase],
            device_id=peer,
            device_id_type=MESH,
        ).start()

    def wait_all(ref, count, sem):
        if count > 0:
            part = ref.at[pl.ds(0, count)]
            pltpu.make_async_copy(part, part, sem).wait()

    barrier = pltpu.get_barrier_semaphore()
    each(1, devices, lambda k: pl.semaphore_signal(barrier, inc=1, device_id=any_peer(k), device_id_type=MESH))
    slot_copy = pltpu.make_async_copy(slot_hbm, slot_ref, local_sem.at[0])
    target_copy = pltpu.make_async_copy(target_hbm, target_ref, local_sem.at[1])
    hidden_copy = pltpu.make_async_copy(hidden_hbm, pieces.at[me], local_sem.at[2])
    final_copy = pltpu.make_async_copy(final_gain_hbm, final_gain_ref.at[0], local_sem.at[3])
    head_copy = pltpu.make_async_copy(head_hbm, head, local_sem.at[4])
    first_copy = pltpu.make_async_copy(first_gain_hbm, first_gain_ref.at[0], local_sem.at[5])
    qkv_copy = pltpu.make_async_copy(qkv_hbm, qkv, local_sem.at[6])
    for copy in (slot_copy, target_copy, hidden_copy, final_copy, head_copy, first_copy, qkv_copy):
        copy.start()
    slot_copy.wait()
    target_copy.wait()
    ids[group, 0:1, 0:row_group] = slot_ref[...]
    ids[group, 1:2, 0:row_group] = target_ref[...]
    hidden_copy.wait()
    pl.semaphore_wait(barrier, devices - 1)

    each(1, groups, lambda k: send(ids.at[group], ids.at[group], 0, group_peer(k)))
    each(1, devices, lambda k: send(pieces.at[me], pieces.at[me], 1, any_peer(k)))

    wait_all(ids, groups - 1, recv_sem.at[0])
    row_iota = lax.broadcasted_iota(jnp.int32, (rows, row_group), 0)
    lane_iota = lax.broadcasted_iota(jnp.int32, (rows, row_group), 1)
    dealt = jnp.zeros((rows, row_group), jnp.float32)
    owned = jnp.zeros((rows, row_group), jnp.float32)
    for k in range(groups):
        slots = ids[k, 0:1, 0:row_group]
        wanted = ids[k, 1:2, 0:row_group].astype(jnp.float32)
        dealt = dealt + jnp.where(row_iota == slots, wanted, 0.0)
        owned = owned + jnp.where(row_iota == lane_iota + k * row_group, wanted, 0.0)
    offset = me * vocab_dev
    vocab_iota = lax.broadcasted_iota(jnp.int32, (rows, vocab_dev), 1) + offset
    dealt_ids = jnp.sum(dealt, axis=1, keepdims=True).astype(jnp.int32)
    owned_ids = jnp.sum(owned, axis=1, keepdims=True).astype(jnp.int32)
    one_hot = jnp.where(dealt_ids == vocab_iota, 1.0, 0.0).astype(jnp.bfloat16)
    head_copy.wait()
    picked[...] = jnp.dot(one_hot, head[...], preferred_element_type=jnp.float32)
    for k in range(groups):
        picked_out[k] = picked[k * row_group : (k + 1) * row_group, :].astype(jnp.bfloat16)

    def columns(v):
        return pl.ds(pl.multiple_of(lax.div(v * tiles, shards) * LANES, LANES), span)

    def send_piece(k):
        peer = lax.rem(me + k, devices)
        peer_group, peer_shard = lax.div(peer, shards), lax.rem(peer, shards)
        send(picked_out.at[peer_group, :, columns(peer_shard)], picked_in.at[me], 3, (peer_group, peer_shard))

    each(1, devices, send_piece)
    picked_in[me] = picked_out[group, :, columns(shard)]

    wait_all(pieces, devices - 1, recv_sem.at[1])
    for k in range(groups):
        for v in range(shards):
            rows_all[k * row_group : (k + 1) * row_group, v * cols : (v + 1) * cols] = pieces[
                k * shards + v
            ].astype(jnp.float32)
    final_copy.wait()
    normed = rms_scaled(rows_all[...], final_gain_ref[...])

    logits = lax.dot_general(
        normed,
        head[...],
        (((1,), (1,)), ((), ())),
        preferred_element_type=jnp.float32,
    )
    top = jnp.max(logits, axis=1, keepdims=True)
    shifted = logits - top
    expons = jnp.exp(shifted)
    columns_of = (
        top,
        jnp.sum(expons, axis=1, keepdims=True),
        jnp.sum(expons * shifted, axis=1, keepdims=True),
        jnp.sum(jnp.where(owned_ids == vocab_iota, logits, 0.0), axis=1, keepdims=True),
    )
    lanes = stats.shape[2]
    diagonal = lax.broadcasted_iota(jnp.int32, (rows, lanes), 0) == lax.broadcasted_iota(
        jnp.int32, (rows, lanes), 1
    )
    put_stats(
        stats,
        me,
        [jnp.sum(jnp.where(diagonal, column, 0.0), axis=0, keepdims=True) for column in columns_of],
    )
    each(1, devices, lambda k: send(stats.at[me], stats.at[me], 2, any_peer(k)))

    wait_all(picked_in, devices - 1, recv_sem.at[3])
    if devices <= UNROLL_MAX:
        total = jnp.sum(picked_in[...].astype(jnp.float32), axis=0)
    else:
        total = lax.fori_loop(
            0,
            devices,
            lambda k, so_far: so_far + picked_in[k].astype(jnp.float32),
            jnp.zeros((row_group, span), jnp.float32),
        )
    summed[shard] = total.astype(jnp.bfloat16)
    each(1, shards, lambda k: send(summed.at[shard], summed.at[shard], 4, shard_peer(k)))


    first_copy.wait()
    qkv_copy.wait()
    wait_all(summed, shards - 1, recv_sem.at[4])
    for v in range(shards):
        embedded[:, starts[v] * LANES : starts[v] * LANES + span] = summed[v].astype(jnp.float32)
    first_normed = rms_scaled(embedded[...], first_gain_ref[...])
    out_ref[...] = jnp.dot(first_normed, qkv[...], preferred_element_type=jnp.float32).astype(out_ref.dtype)

    wait_all(stats, devices - 1, recv_sem.at[2])
    row_top, row_total, row_weighted, row_target = merged(stats)
    log_total = jnp.log(row_total)
    logprob = row_target - row_top - log_total
    entropy = log_total - row_weighted / row_total
    for ref, values in ((logprob_ref, logprob), (entropy_ref, entropy)):
        mine = values[:, 0:row_group]
        for k in range(1, groups):
            mine = jnp.where(group == k, values[:, k * row_group : (k + 1) * row_group], mine)
        ref[...] = mine

    wait_all(ids, groups - 1, send_sem.at[0])
    wait_all(pieces, devices - 1, send_sem.at[1])
    wait_all(picked_in, devices - 1, send_sem.at[3])
    wait_all(stats, devices - 1, send_sem.at[2])
    wait_all(summed, shards - 1, send_sem.at[4])


def hand_over(*refs):
    sems = refs[-1]
    copies = [pltpu.make_async_copy(refs[k], refs[k + 3], sems.at[k]) for k in range(3)]
    for copy in copies:
        copy.start()
    for copy in copies:
        copy.wait()


def local(groups, shards, hidden, dealt_slot, targets, final_gain, vocab_head, first_gain, qkv_weight):
    row_group, cols = hidden.shape
    rows = row_group * groups
    width_all = vocab_head.shape[1]
    tiles = width_all // LANES
    starts = [v * tiles // shards for v in range(shards)]
    width = max(b - a for a, b in zip(starts, starts[1:] + [tiles]))
    span = width * LANES
    lanes = -(-rows // LANES) * LANES
    qkv_cols = qkv_weight.shape[1]
    vmem = pl.BlockSpec(memory_space=pltpu.VMEM)
    hbm = pl.BlockSpec(memory_space=pltpu.HBM)
    logprob, entropy, projected = pl.pallas_call(
        functools.partial(kernel, groups, shards, starts, width),
        out_shape=(
            pltpu.VMEM((1, row_group), jnp.float32),
            pltpu.VMEM((1, row_group), jnp.float32),
            pltpu.VMEM((row_group, qkv_cols), jnp.bfloat16),
        ),
        in_specs=[hbm] * 7,
        out_specs=(vmem, vmem, vmem),
        scratch_shapes=[
            pltpu.VMEM(vocab_head.shape, jnp.bfloat16),
            pltpu.VMEM(qkv_weight.shape, jnp.bfloat16),
            pltpu.VMEM((1, row_group), jnp.int32),
            pltpu.VMEM((1, row_group), jnp.int32),
            pltpu.VMEM((1, width_all), jnp.float32),
            pltpu.VMEM((1, width_all), jnp.float32),
            pltpu.VMEM((groups, 8, LANES), jnp.int32),
            pltpu.VMEM((groups * shards, row_group, cols), jnp.bfloat16),
            pltpu.VMEM((rows, width_all), jnp.float32),
            pltpu.VMEM((rows, width_all), jnp.float32),
            pltpu.VMEM((groups, row_group, width_all), jnp.bfloat16),
            pltpu.VMEM((groups * shards, row_group, span), jnp.bfloat16),
            pltpu.VMEM((shards, row_group, span), jnp.bfloat16),
            pltpu.VMEM((row_group, width_all), jnp.float32),
            pltpu.VMEM((groups * shards, 4, lanes), jnp.float32),
            pltpu.SemaphoreType.DMA((7,)),
            pltpu.SemaphoreType.DMA((5,)),
            pltpu.SemaphoreType.DMA((5,)),
        ],
        compiler_params=pltpu.CompilerParams(
            collective_id=0, has_side_effects=True, vmem_limit_bytes=63 * 1024 * 1024
        ),
    )(
        hidden,
        dealt_slot.reshape(1, row_group),
        targets.reshape(1, row_group),
        final_gain,
        vocab_head,
        first_gain,
        qkv_weight,
    )
    results = [pltpu.with_memory_space_constraint(r, pltpu.VMEM) for r in (logprob, entropy, projected)]
    logprob, entropy, projected = pl.pallas_call(
        hand_over,
        out_shape=tuple(jax.ShapeDtypeStruct(r.shape, r.dtype) for r in results),
        in_specs=[pl.BlockSpec(memory_space=pltpu.VMEM)] * 3,
        out_specs=(hbm,) * 3,
        scratch_shapes=[pltpu.SemaphoreType.DMA((3,))],
    )(*results)
    return (logprob.reshape(row_group), entropy.reshape(row_group), projected.T)


def solution(mesh):
    return jax.shard_map(
        functools.partial(local, mesh.shape["group"], mesh.shape["vocab"]),
        mesh=mesh,
        in_specs=(
            P("group", "vocab"),
            P("group"),
            P("group"),
            P(),
            P(("group", "vocab"), None),
            P(),
            P(None, "vocab"),
        ),
        out_specs=(P("group"), P("group"), P("vocab", "group")),
        check_vma=False,
    )
```
